128 devices in a mesh: dp: 4 (over y), slab: 32 (over z, x, core).
Axes of the slice: x: 4, y: 4, z: 4, core: 2. Of those that a mesh axis runs over, the one named last changes fastest.
Arguments:
- grad_out: bfloat16 [4, 32, 128, 128, 128], P('dp', None, 'slab'), may hold values from -6 to 6
- pre_act: bfloat16 [4, 32, 128, 128, 128], P('dp', None, 'slab'), may hold values from -9 to 9
- forward_modes: bfloat16 [4, 32, 2, 32, 512], P('dp', 'slab'), may hold values from -6 to 6
- spec_weight: bfloat16 [32, 2, 32, 32, 512], P('slab', None, None, 'dp'), may hold values from -18 to 18
- w_local: bfloat16 [32, 32], replicated, may hold values from -1 to 1
Outputs:
- grad_in: bfloat16 [4, 32, 128, 128, 128], P('dp', None, 'slab')
- spec_weight_grad: float32 [32, 2, 32, 32, 512], P('slab', None, None, 'dp')
The draws below stay inside these ranges and needn't reach their ends.
All inputs are finite; a program needn't handle non-finite values.
Results may differ from the reference program's by a relative error of at most 0.014.
Values may be sent and summed in bfloat16 or wider, within the bound.
No kernel may reach another device: no remote copies, remote signals or barrier semaphores. Data moves between devices by JAX's collectives and lax.ppermute only.
A program may use at most 128 MiB of HBM per device.

```python
import math
import jax
import jax.numpy as jnp
from jax import lax

C = 32
NY = 128
NZ = 128
KY = 32
KZ = 16
KX = 32
NX = 128
BATCH = 4


def block_levels(rng, dims, split, low, top_value):
    def one(axis_at, shards_of):
        draws = jax.random.uniform(jax.random.fold_in(jax.random.fold_in(rng, 6), axis_at), (shards_of,), jnp.float32, low / len(split), top_value / len(split))
        return jnp.repeat(jnp.exp(draws), dims[axis_at] // shards_of).reshape((-1,) + (1,) * (len(dims) - axis_at - 1))

    level = one(*split[0])
    for cut in split[1:]:
        level = level * one(*cut)
    return level


def noise(key, extent, width, reach, cuts=(), kind=jnp.bfloat16):
    entries = jax.random.normal(key, extent, jnp.float32) * width
    if len(cuts) > 0:
        entries = block_levels(key, extent, cuts, -0.22, 0.18) * entries
    return jnp.clip(entries, min=-reach, max=reach).astype(kind)


def setup_inputs(seed: int = 0) -> dict:
    splits = jax.random.split(jax.random.key(seed), 6)
    grad_out = noise(splits[0], (BATCH, C, NX, NY, NZ), 1.0, 6.0, ((0, 4), (2, 32)))
    pre_act = noise(splits[1], (BATCH, C, NX, NY, NZ), 1.5, 9.0, ((0, 4), (2, 32)))
    forward_modes = noise(splits[2], (BATCH, KX, 2, C, KY * KZ), 1.0, 6.0, ((0, 4), (1, 32)))
    spec_weight = noise(splits[3], (KX, 2, C, C, KY * KZ), 3.0, 18.0, ((0, 32), (3, 4)))
    w_local = noise(splits[4], (C, C), C ** -0.5, 1.0)
    return {"grad_out": grad_out, "pre_act": pre_act, "forward_modes": forward_modes, "spec_weight": spec_weight, "w_local": w_local}


def gelu_slope(value):
    cdf = 0.5 * (1.0 + lax.erf(value * 0.7071067811865476))
    return cdf + value * jnp.exp(-0.5 * value * value) * 0.3989422804014327

def kept_modes(count, length):
    index = jnp.arange(count, dtype=jnp.int32)
    return jnp.where(index < count // 2, index, length - count + index)

def angle_table(modes, cells, length):
    product = modes[:, None] * cells[None, :] % length
    return product.astype(jnp.float32) * (2.0 * math.pi / length)

def z_tables():
    modes = jnp.arange(KZ, dtype=jnp.int32)
    angles = angle_table(modes, jnp.arange(NZ, dtype=jnp.int32), NZ)
    weight = jnp.where(modes == 0, 1.0, 2.0).astype(jnp.float32)[:, None]
    scale = 1.0 / math.sqrt(NY * NZ)
    analysis = jnp.concatenate([jnp.cos(angles) * weight, -jnp.sin(angles) * weight], 0).T * scale
    synthesis = jnp.concatenate([jnp.cos(angles), -jnp.sin(angles)], 0) * scale
    return (analysis.astype(jnp.bfloat16), synthesis)

def y_tables():
    angles = angle_table(kept_modes(KY, NY), jnp.arange(NY, dtype=jnp.int32), NY)
    return (jnp.cos(angles), jnp.sin(angles))

def x_tables():
    angles = angle_table(kept_modes(KX, NX), jnp.arange(NX, dtype=jnp.int32), NX)
    scale = 1.0 / math.sqrt(NX)
    return (jnp.cos(angles) * scale, jnp.sin(angles) * scale)

def one_sample(grad_sample, pre_sample, modes_sample, spec_weight, w_local):
    high = lax.Precision.HIGHEST
    za, zs = z_tables()
    cy, sy = y_tables()
    cx, sx = x_tables()
    dpre = (grad_sample.astype(jnp.float32) * gelu_slope(pre_sample.astype(jnp.float32))).astype(jnp.bfloat16)
    z_part = jnp.dot(dpre.reshape(-1, NZ), za, preferred_element_type=jnp.float32).reshape(C, NX, NY, 2, KZ)
    zr, zi = (z_part[:, :, :, 0], z_part[:, :, :, 1])
    pr = jnp.einsum('cxyk,qy->xcqk', zr, cy, precision=high) + jnp.einsum('cxyk,qy->xcqk', zi, sy, precision=high)
    pim = jnp.einsum('cxyk,qy->xcqk', zi, cy, precision=high) - jnp.einsum('cxyk,qy->xcqk', zr, sy, precision=high)
    proj = jnp.stack([pr, pim], 1).reshape(NX, 2, C, KY * KZ).astype(jnp.bfloat16).astype(jnp.float32)
    gr = jnp.einsum('jx,xcm->jcm', cx, proj[:, 0], precision=high) + jnp.einsum('jx,xcm->jcm', sx, proj[:, 1], precision=high)
    gi = jnp.einsum('jx,xcm->jcm', cx, proj[:, 1], precision=high) - jnp.einsum('jx,xcm->jcm', sx, proj[:, 0], precision=high)
    saved = modes_sample.astype(jnp.float32)
    ur, ui = (saved[:, 0], saved[:, 1])
    wr = jnp.einsum('jom,jim->jiom', gr, ur, precision=high) + jnp.einsum('jom,jim->jiom', gi, ui, precision=high)
    wi = jnp.einsum('jom,jim->jiom', gi, ur, precision=high) - jnp.einsum('jom,jim->jiom', gr, ui, precision=high)
    weights = spec_weight.astype(jnp.float32)
    vr, vi = (weights[:, 0], weights[:, 1])
    dr = jnp.einsum('jom,jiom->jim', gr, vr, precision=high) + jnp.einsum('jom,jiom->jim', gi, vi, precision=high)
    di = jnp.einsum('jom,jiom->jim', gi, vr, precision=high) - jnp.einsum('jom,jiom->jim', gr, vi, precision=high)
    back = jnp.stack([dr, di], 1).astype(jnp.bfloat16).astype(jnp.float32)
    br, bi = (back[:, 0], back[:, 1])
    xr = jnp.einsum('jx,jcm->xcm', cx, br, precision=high) - jnp.einsum('jx,jcm->xcm', sx, bi, precision=high)
    xi = jnp.einsum('jx,jcm->xcm', cx, bi, precision=high) + jnp.einsum('jx,jcm->xcm', sx, br, precision=high)
    xr = xr.reshape(NX, C, KY, KZ)
    xi = xi.reshape(NX, C, KY, KZ)
    yr = jnp.einsum('xcqk,qy->cxyk', xr, cy, precision=high) - jnp.einsum('xcqk,qy->cxyk', xi, sy, precision=high)
    yi = jnp.einsum('xcqk,qy->cxyk', xi, cy, precision=high) + jnp.einsum('xcqk,qy->cxyk', xr, sy, precision=high)
    spectral = jnp.dot(jnp.concatenate([yr, yi], -1).reshape(-1, 2 * KZ), zs, precision=high)
    local = jnp.dot(w_local, dpre.reshape(C, -1), preferred_element_type=jnp.float32)
    total = spectral.reshape(C, NX, NY, NZ) + local.reshape(C, NX, NY, NZ)
    return (total.astype(jnp.bfloat16), jnp.stack([wr, wi], 1))

def reference(grad_out, pre_act, forward_modes, spec_weight, w_local):

    def step(items):
        return one_sample(items[0], items[1], items[2], spec_weight, w_local)
    grad_in, terms = lax.map(step, (grad_out, pre_act, forward_modes))
    return (grad_in, lax.optimization_barrier(jnp.sum(terms, axis=0)))
```

```python
import math

import jax
import jax.numpy as jnp
import numpy as np
from jax import lax
from jax.sharding import PartitionSpec as P

KX = 32
KY = 32
KZ = 16
KH = 4
KL = 4
ALL = ("dp", "slab")
BF = jnp.bfloat16
F32 = jnp.float32


def kept(count, length):
    index = np.arange(count)
    return np.where(index < count // 2, index, length - count + index)


def angles(modes, length):
    return (modes[:, None] * np.arange(length)[None, :] % length) * (2.0 * math.pi / length)


def z_analysis(ny, nz):
    ang = angles(np.arange(KZ), nz)
    weight = np.where(np.arange(KZ) == 0, 1.0, 2.0)[:, None]
    scale = 1.0 / math.sqrt(ny * nz)
    real, imag = (np.cos(ang) * weight * scale).T, (-np.sin(ang) * weight * scale).T
    return real, imag


def x_table(nx):
    ang = angles(kept(KX, nx), nx)
    scale = 1.0 / math.sqrt(nx)
    cos, sin = np.cos(ang) * scale, np.sin(ang) * scale
    out = np.zeros((nx, 2, 2, KX))
    out[:, 0, 0], out[:, 0, 1] = cos.T, -sin.T
    out[:, 1, 0], out[:, 1, 1] = sin.T, cos.T
    return out


def bf(table):
    return jnp.asarray(table, F32).astype(BF)


def gelu_slope(value):
    cdf = 0.5 * (1.0 + lax.erf(value * 0.7071067811865476))
    return cdf + value * jnp.exp(-0.5 * value * value) * 0.3989422804014327


def dot(spec, left, right):
    return jnp.einsum(spec, left, right, preferred_element_type=F32)


def shards(grad_out, pre_act, forward_modes, spec_weight, w_local):
    _, chans, planes, ny, nz = grad_out.shape
    dps, slabs = lax.axis_size("dp"), lax.axis_size("slab")
    nx = planes * slabs
    devs = dps * slabs
    share = chans // dps
    me = lax.axis_index("dp")

    vs = spec_weight.reshape(2, chans, share, devs, KL)
    vs = vs.transpose(3, 4, 0, 1, 2).reshape(devs, 16, 128)
    vs = lax.all_to_all(vs, ALL, 0, 0, tiled=True)
    vs = vs.reshape(dps, slabs, KL, 2, chans, share).transpose(3, 4, 0, 5, 1, 2)
    vs = vs.reshape(2, chans, chans, slabs * KL).astype(F32)

    fm = forward_modes.reshape(2, chans, KY * KZ)
    fms = [fm]
    for hop in range(1, dps):
        fms.append(lax.ppermute(fm, "dp", [(i, i ^ hop) for i in range(dps)]))

    dpre = (grad_out.astype(F32) * gelu_slope(pre_act.astype(F32))).astype(BF)[0]
    zr, zi = z_analysis(ny, nz)
    za = bf(np.stack([np.concatenate([zr, zi], 1), np.concatenate([zi, -zr], 1)], 1).reshape(nz, -1))
    tz = dot("cpyz,zk->cpyk", dpre, za).astype(BF).reshape(chans, planes, ny, 2, 2 * KZ)
    ang = angles(kept(KY, ny), ny)
    cs = bf(np.stack([np.cos(ang).T, np.sin(ang).T], 1))
    proj = dot("cpyhk,yhq->cpqk", tz, cs).astype(BF)
    proj = proj.reshape(chans, planes, KY, 2, KH, KL).transpose(2, 4, 1, 3, 5, 0)
    proj = proj.reshape(devs, planes * 2, KL * chans)
    got = lax.all_to_all(proj, ALL, 0, 0, tiled=True)
    got = got.reshape(dps, slabs * planes * 2, KL, chans)
    wx = x_table(nx)
    grad = dot("bxlo,xrj->brojl", got, bf(wx.reshape(nx * 2, 2, KX)))
    grad = grad.reshape(dps, 2, chans, KX * KL)
    gr, gi = grad[:, 0], grad[:, 1]

    def mix(left, right):
        return jnp.sum(left[:, None] * right[None], 2)

    back_r = mix(gr, vs[0]) + mix(gi, vs[1])
    back_i = mix(gi, vs[0]) - mix(gr, vs[1])
    back = jnp.stack([back_r, back_i], 1).astype(BF).reshape(dps, 2, chans, KX, KL)
    wi = bf(wx.transpose(2, 3, 0, 1).reshape(2, KX, nx * 2))
    xp = dot("brijl,rjx->bxli", back, wi).astype(BF)
    xp = xp.reshape(devs, planes * 2, KL * chans)
    gt = grad.astype(BF).reshape(dps, 2, chans, KX, KL).transpose(3, 1, 4, 0, 2).reshape(1, KX, 8, 128)
    gt = jnp.broadcast_to(gt, (dps, KX, 8, 128)).reshape(devs, 8, 128)
    got = lax.all_to_all(jnp.concatenate([xp, gt], 1), ALL, 0, 0, tiled=True)

    local = dot("io,opyz->ipyz", w_local, dpre)

    xq = got[:, :8].reshape(KY, KH, planes, 2, KL, chans).transpose(5, 2, 0, 3, 1, 4)
    xq = xq.reshape(chans, planes, KY, 2 * KZ)
    uv = dot("cpqk,yhq->cpyhk", xq, cs).astype(BF).reshape(chans, planes, ny, 4 * KZ)
    zang = angles(np.arange(KZ), nz)
    scale = 1.0 / math.sqrt(ny * nz)
    cz, sz = np.cos(zang) * scale, np.sin(zang) * scale
    zs = bf(np.concatenate([cz, -sz, -sz, -cz], 0))
    grad_in = (dot("cpyk,kz->cpyz", uv, zs) + local).astype(BF)[None]

    gm = got[:, 8:].reshape(devs, 2, KL, dps, dps, share)
    gm = lax.dynamic_index_in_dim(gm, me, 4, keepdims=False)
    gm = gm.transpose(3, 1, 4, 0, 2).reshape(dps, 2, share, KY * KZ).astype(F32)
    wr, wi_ = 0.0, 0.0
    for hop in range(dps):
        g = lax.dynamic_index_in_dim(gm, me ^ hop, 0, keepdims=False)
        u = fms[hop].astype(F32)
        g_r, g_i, u_r, u_i = g[0][None], g[1][None], u[0][:, None], u[1][:, None]
        wr = wr + g_r * u_r + g_i * u_i
        wi_ = wi_ + g_i * u_r - g_r * u_i
    spec_grad = jnp.stack([wr, wi_], 0)[None]
    return (grad_in, spec_grad)


def solution(mesh):
    return jax.shard_map(
        shards,
        mesh=mesh,
        in_specs=(
            P("dp", None, "slab", None, None),
            P("dp", None, "slab", None, None),
            P("dp", "slab", None, None, None),
            P("slab", None, None, "dp", None),
            P(),
        ),
        out_specs=(P("dp", None, "slab", None, None), P("slab", None, None, "dp", None)),
        check_vma=False,
    )
```

```python
import functools
import math

import jax
import jax.numpy as jnp
import numpy as np
from jax import lax
from jax.experimental import pallas as pl
from jax.experimental.pallas import tpu as pltpu
from jax.sharding import PartitionSpec as P

C = 32
NP = 4
NY = 128
NZ = 128
KX = 32
KY = 32
KZ = 16
NB = 4
NS = 32
QL = 4
SHARE = C // NB
DEVS = NB * NS
STEPS = 8
CB = C // STEPS
ALL = ("dp", "slab")
BF = jnp.bfloat16
F32 = jnp.float32
VMEM_LIMIT = 56 * 1024 * 1024


def kept(count, length):
    index = np.arange(count)
    return np.where(index < count // 2, index, length - count + index)


def angles(modes, length):
    return (modes[:, None] * np.arange(length)[None, :] % length) * (2.0 * math.pi / length)


def bf(table):
    return jnp.asarray(table, F32).astype(BF)


@functools.cache
def z_analysis():
    ang = angles(np.arange(KZ), NZ)
    weight = np.where(np.arange(KZ) == 0, 1.0, 2.0)[:, None] / math.sqrt(NY * NZ)
    real, imag = (np.cos(ang) * weight).T, (-np.sin(ang) * weight).T
    out = np.zeros((NP, NZ, 2, KZ, NP, 2), np.float32)
    for p in range(NP):
        out[p, :, 0, :, p, 0], out[p, :, 0, :, p, 1] = real, imag
        out[p, :, 1, :, p, 0], out[p, :, 1, :, p, 1] = imag, -real
    return out.reshape(NP * NZ, 2 * 128)


@functools.cache
def z_synthesis():
    ang = angles(np.arange(KZ), NZ)
    scale = 1.0 / math.sqrt(NY * NZ)
    cos, sin = np.cos(ang) * scale, np.sin(ang) * scale
    out = np.zeros((2, KZ, NP, 2, NP, NZ), np.float32)
    for p in range(NP):
        out[0, :, p, 0, p], out[0, :, p, 1, p] = cos, -sin
        out[1, :, p, 0, p], out[1, :, p, 1, p] = -sin, -cos
    return out.reshape(2 * 128, NP * NZ)


@functools.cache
def y_table():
    ang = angles(kept(KY, NY), NY)
    return np.concatenate([np.cos(ang), np.sin(ang)], 0).astype(np.float32)


@functools.cache
def x_table():
    nx = NS * NP
    ang = angles(kept(KX, nx), nx)
    cos, sin = np.cos(ang).T / math.sqrt(nx), np.sin(ang).T / math.sqrt(nx)
    out = np.zeros((nx, 2, 2, KX), np.float32)
    out[:, 0, 0], out[:, 0, 1], out[:, 1, 0], out[:, 1, 1] = cos, -sin, sin, cos
    return out


@functools.cache
def x_forward():
    out = np.zeros((QL, NS * NP, 2, 2, QL, KX), np.float32)
    for ql in range(QL):
        out[ql, :, :, :, ql] = x_table()
    return out.reshape(QL, 256, 256)


@functools.cache
def x_inverse():
    out = np.zeros((QL, 2, QL, KX, NS * NP, 2), np.float32)
    for ql in range(QL):
        out[ql, :, ql] = x_table().transpose(2, 3, 0, 1)
    return out.reshape(QL, 256, 256)


def dot(left, right):
    return jnp.dot(left, right, preferred_element_type=F32)


def gelu_slope(x):
    a = jnp.abs(x)
    t = pl.reciprocal(1.0 + (0.3275911 * math.sqrt(0.5)) * a, approx=True)
    poly = 0.5 * 1.061405429 * t + 0.5 * -1.453152027
    poly = poly * t + 0.5 * 1.421413741
    poly = poly * t + 0.5 * -0.284496736
    poly = poly * t + 0.5 * 0.254829592
    tail = jnp.exp2(x * x * (-0.5 * math.log2(math.e))) * (poly * t - 0.3989422804014327 * a)
    return jnp.where(x >= 0.0, 1.0 - tail, tail)


def analysis_kernel(go_ref, pa_ref, sw_ref, za_ref, cs_ref, dpre_ref, send_ref, proj_ref, rows_ref):
    step = pl.program_id(0)
    for c in range(CB):
        parts = []
        for p in range(NP):
            value = go_ref[0, c, p].astype(F32) * gelu_slope(pa_ref[0, c, p].astype(F32))
            parts.append(value.astype(BF))
            dpre_ref[c, p] = parts[-1]
        tz = dot(jnp.concatenate(parts[:2], 1), za_ref[:256])
        tz = (tz + dot(jnp.concatenate(parts[2:], 1), za_ref[256:])).astype(BF)
        both = dot(cs_ref[...], tz)
        proj_ref[pl.ds((step * CB + c) * KY, KY), :] = both[:KY, :128] + both[KY:, 128:]

    block = sw_ref[0, 0].astype(F32).reshape(128, 256)
    j = step // 2
    for h in range(2):
        turned = block[:, h * 128 : (h + 1) * 128].T
        for qh in range(2):
            first = ((step % 2) * 4 + h * 2 + qh) * KZ
            for ql in range(QL):
                at = (qh * QL + ql) * KZ
                rows_ref[pl.ds(first * 24 + 8 + j * 4 + ql, KZ, stride=24), :] = turned[at : at + KZ]

    @pl.when(step == STEPS - 1)
    def _():
        for qh in range(KY // QL):
            group = [proj_ref[pl.ds(qh * QL + ql, C, stride=KY), :] for ql in range(QL)]
            turned = jnp.concatenate(group, 0).T
            for kz in range(KZ):
                rows_ref[pl.ds((qh * KZ + kz) * 24, 8), :] = turned[kz * 8 : kz * 8 + 8]
        send_ref[...] = rows_ref[...].reshape(DEVS, 24, 128).astype(BF)


def analysis(grad_out, pre_act, spec_weight):
    whole = lambda *shape: pl.BlockSpec(shape, lambda n: (0,) * len(shape))
    return pl.pallas_call(
        analysis_kernel,
        grid=(STEPS,),
        in_specs=[
            pl.BlockSpec((1, CB, NP, NY, NZ), lambda n: (0, n, 0, 0, 0)),
            pl.BlockSpec((1, CB, NP, NY, NZ), lambda n: (0, n, 0, 0, 0)),
            pl.BlockSpec((1, 1, 16, SHARE, 256), lambda n: (0, n // 4, (n // 2) % 2, 0, n % 2)),
            whole(NP * NZ, 256),
            whole(2 * KY, NY),
        ],
        out_specs=[
            pl.BlockSpec((CB, NP, NY, NZ), lambda n: (n, 0, 0, 0)),
            whole(DEVS, 24, 128),
        ],
        out_shape=[
            jax.ShapeDtypeStruct((C, NP, NY, NZ), BF),
            jax.ShapeDtypeStruct((DEVS, 24, 128), BF),
        ],
        scratch_shapes=[pltpu.VMEM((C * KY, 128), F32), pltpu.VMEM((DEVS * 24, 128), F32)],
        compiler_params=pltpu.CompilerParams(vmem_limit_bytes=VMEM_LIMIT),
        name="analysis",
    )(grad_out, pre_act, spec_weight, bf(z_analysis()), bf(y_table()))


def mix_kernel(got_ref, wf_ref, wi_ref, send_ref, rows_ref, v_ref, out_ref, g_ref, back_ref):
    rows_ref[...] = got_ref[...].astype(F32).reshape(DEVS * 24, 128)
    for j in range(4):
        for og in range(NB):
            first = og * NS * 24 + 8 + j * 4
            group = [rows_ref[pl.ds(first + ql, KX, stride=24), :] for ql in range(QL)]
            at = (j * NB + og) * 128
            v_ref[at : at + 128, :] = jnp.concatenate(group, 0).T

    planes = []
    for b in range(NB):
        part = [rows_ref[pl.ds((b * NS + s) * 24, 8), :] for s in range(NS)]
        planes.append(jnp.concatenate(part, 0).T.astype(BF))
    grad = jnp.zeros((NB * C, 256), F32)
    for ql in range(QL):
        left = jnp.concatenate([planes[b][ql * C : (ql + 1) * C] for b in range(NB)], 0)
        grad = grad + dot(left, wf_ref[ql])
    g_ref[...] = grad

    turned = grad.T
    for r in range(2):
        for ql in range(QL):
            at = (r * QL + ql) * KX
            for og in range(NB):
                first = og * NS * 16 + 8 + r * QL + ql
                out_ref[pl.ds(first, KX, stride=16), :] = turned[at : at + KX]

    for ig in range(4):
        acc = [[jnp.zeros((8, 128), F32) for _ in range(2)] for _ in range(NB)]
        for o in range(C):
            at = (o // SHARE) * 128 + (ig % 2) * 64 + o % SHARE
            vr = v_ref[pl.ds((ig // 2) * 512 + at, 8, stride=SHARE), :]
            vi = v_ref[pl.ds((2 + ig // 2) * 512 + at, 8, stride=SHARE), :]
            for b in range(NB):
                gr = g_ref[pl.ds(b * C + o, 1), :128]
                gi = g_ref[pl.ds(b * C + o, 1), 128:]
                acc[b][0] = acc[b][0] + gr * vr + gi * vi
                acc[b][1] = acc[b][1] + gi * vr - gr * vi
        for b in range(NB):
            back_ref[b * C + ig * 8 : b * C + ig * 8 + 8, :] = jnp.concatenate(acc[b], 1)

    back = back_ref[...].astype(BF)
    outs = [dot(back, wi_ref[ql]) for ql in range(QL)]
    for b in range(NB):
        turned = jnp.concatenate([outs[ql][b * C : (b + 1) * C] for ql in range(QL)], 0).T
        for s in range(NS):
            out_ref[pl.ds((b * NS + s) * 16, 8), :] = turned[s * 8 : s * 8 + 8]
    send_ref[...] = out_ref[...].reshape(DEVS, 16, 128).astype(BF)


def mix(got):
    return pl.pallas_call(
        mix_kernel,
        out_shape=jax.ShapeDtypeStruct((DEVS, 16, 128), BF),
        scratch_shapes=[
            pltpu.VMEM((DEVS * 24, 128), F32),
            pltpu.VMEM((16 * 128, 128), F32),
            pltpu.VMEM((DEVS * 16, 128), F32),
            pltpu.VMEM((128, 256), F32),
            pltpu.VMEM((128, 256), F32),
        ],
        compiler_params=pltpu.CompilerParams(vmem_limit_bytes=VMEM_LIMIT),
        name="mix",
    )(got, bf(x_forward()), bf(x_inverse()))


def synthesis_kernel(me_ref, got_ref, local_ref, fm0, fm1, fm2, fm3, cs_ref, zs_ref, out_ref, spec_ref, rows_ref, x_ref, g_ref, u_ref):
    step = pl.program_id(0)
    me = me_ref[0]

    @pl.when(step == 0)
    def _():
        rows_ref[...] = got_ref[...].astype(F32).reshape(DEVS * 16, 128)
        for qh in range(KY // QL):
            group = [rows_ref[pl.ds((qh * KZ + kz) * 16, 8), :] for kz in range(KZ)]
            turned = jnp.concatenate(group, 0).T
            for ql in range(QL):
                x_ref[pl.ds(qh * QL + ql, C, stride=KY), :] = turned[ql * C : (ql + 1) * C]
        for r in range(2):
            for tile in range(4):
                group = []
                for q in range(2 * QL):
                    first = (tile * 2 + q // QL) * KZ * 16 + 8 + r * QL + q % QL
                    group.append(rows_ref[pl.ds(first, KZ, stride=16), :])
                g_ref[r, :, tile * 128 : (tile + 1) * 128] = jnp.concatenate(group, 0).T
        for hop, fm in enumerate((fm0, fm1, fm2, fm3)):
            u_ref[hop] = fm[...].astype(F32)

    for pair in range(CB // 2):
        first = (step * CB + pair * 2) * KY
        xs = jnp.concatenate([x_ref[pl.ds(first, KY), :], x_ref[pl.ds(first + KY, KY), :]], 1)
        uv = dot(cs_ref[...], xs.astype(BF)).astype(BF)
        for k in range(2):
            left = jnp.concatenate([uv[:NY, k * 128 : k * 128 + 128], uv[NY:, k * 128 : k * 128 + 128]], 1)
            full = dot(left, zs_ref[...])
            for p in range(NP):
                c = pair * 2 + k
                total = full[:, p * NZ : (p + 1) * NZ] + local_ref[c, p].astype(F32)
                out_ref[0, c, p] = total.astype(BF)

    for k in range(CB):
        i = step * CB + k
        wr, wi = jnp.zeros((SHARE, KY * KZ), F32), jnp.zeros((SHARE, KY * KZ), F32)
        for hop in range(NB):
            at = pl.multiple_of((me ^ hop) * C + me * SHARE, SHARE)
            gr, gi = g_ref[0, pl.ds(at, SHARE), :], g_ref[1, pl.ds(at, SHARE), :]
            ur, ui = u_ref[hop, 0, pl.ds(i, 1), :], u_ref[hop, 1, pl.ds(i, 1), :]
            wr = wr + gr * ur + gi * ui
            wi = wi + gi * ur - gr * ui
        spec_ref[0, 0, k] = wr
        spec_ref[0, 1, k] = wi


def synthesis(me, got, local, fms):
    whole = lambda *shape: pl.BlockSpec(shape, lambda n: (0,) * len(shape))
    table = y_table().reshape(2, KY, NY).transpose(0, 2, 1).reshape(2 * NY, KY)
    return pl.pallas_call(
        synthesis_kernel,
        grid=(STEPS,),
        in_specs=[
            pl.BlockSpec(memory_space=pltpu.SMEM),
            whole(DEVS, 16, 128),
            pl.BlockSpec((CB, NP, NY, NZ), lambda n: (n, 0, 0, 0)),
            *[whole(2, C, KY * KZ)] * NB,
            whole(2 * NY, KY),
            whole(256, NP * NZ),
        ],
        out_specs=[
            pl.BlockSpec((1, CB, NP, NY, NZ), lambda n: (0, n, 0, 0, 0)),
            pl.BlockSpec((1, 2, CB, SHARE, KY * KZ), lambda n: (0, 0, n, 0, 0)),
        ],
        out_shape=[
            jax.ShapeDtypeStruct((1, C, NP, NY, NZ), BF),
            jax.ShapeDtypeStruct((1, 2, C, SHARE, KY * KZ), F32),
        ],
        scratch_shapes=[
            pltpu.VMEM((DEVS * 16, 128), F32),
            pltpu.VMEM((C * KY, 128), F32),
            pltpu.VMEM((2, 128, KY * KZ), F32),
            pltpu.VMEM((NB, 2, C, KY * KZ), F32),
        ],
        compiler_params=pltpu.CompilerParams(vmem_limit_bytes=VMEM_LIMIT),
        name="synthesis",
    )(me, got, local, *fms, bf(table), bf(z_synthesis()))


def shards(grad_out, pre_act, forward_modes, spec_weight, w_local):
    me = lax.axis_index("dp")
    dpre, send = analysis(grad_out, pre_act, spec_weight)
    got = lax.all_to_all(send, ALL, 0, 0, tiled=True)
    fm = forward_modes.reshape(2, C, KY * KZ)
    fms = [fm] + [lax.ppermute(fm, "dp", [(b, b ^ hop) for b in range(NB)]) for hop in range(1, NB)]
    local = jnp.einsum("io,opyz->ipyz", w_local, dpre, preferred_element_type=F32).astype(BF)
    got = lax.all_to_all(mix(got), ALL, 0, 0, tiled=True)
    return synthesis(me.reshape(1), got, local, fms)


def solution(mesh):
    return jax.shard_map(
        shards,
        mesh=mesh,
        in_specs=(
            P("dp", None, "slab", None, None),
            P("dp", None, "slab", None, None),
            P("dp", "slab", None, None, None),
            P("slab", None, None, "dp", None),
            P(),
        ),
        out_specs=(P("dp", None, "slab", None, None), P("slab", None, None, "dp", None)),
        check_vma=False,
    )
```

```python
import functools
import math

import jax
import jax.numpy as jnp
import numpy as np
from jax import lax
from jax.experimental import pallas as pl
from jax.experimental.pallas import tpu as pltpu
from jax.sharding import PartitionSpec as P

C = 32
NP = 4
NY = 128
NZ = 128
KX = 32
KY = 32
KZ = 16
NB = 4
NS = 32
QL = 4
SHARE = C // NB
DEVS = NB * NS
STEPS = 8
CB = C // STEPS
AHEAD = 3
ALL = ("dp", "slab")
BF = jnp.bfloat16
F32 = jnp.float32
VMEM_LIMIT = 56 << 20


def kept(count, length):
    index = np.arange(count)
    return np.where(index < count // 2, index, length - count + index)


def angles(modes, length):
    return (modes[:, None] * np.arange(length)[None, :] % length) * (2.0 * math.pi / length)


def bf(table):
    return jnp.asarray(table, F32).astype(BF)


@functools.cache
def z_analysis():
    ang = angles(np.arange(KZ), NZ)
    weight = np.where(np.arange(KZ) == 0, 0.5, 1.0)[:, None] / math.sqrt(NY * NZ)
    real, imag = (np.cos(ang) * weight).T, (-np.sin(ang) * weight).T
    out = np.zeros((NP, NZ, 2, KZ, NP, 2), np.float32)
    for p in range(NP):
        out[p, :, 0, :, p, 0], out[p, :, 0, :, p, 1] = real, imag
        out[p, :, 1, :, p, 0], out[p, :, 1, :, p, 1] = imag, -real
    return out.reshape(NP * NZ, 2 * 128)


@functools.cache
def z_synthesis():
    ang = angles(np.arange(KZ), NZ)
    scale = 1.0 / math.sqrt(NY * NZ)
    cos, sin = np.cos(ang) * scale, np.sin(ang) * scale
    out = np.zeros((2, KZ, NP, 2, NP, NZ), np.float32)
    for p in range(NP):
        out[0, :, p, 0, p], out[0, :, p, 1, p] = cos, -sin
        out[1, :, p, 0, p], out[1, :, p, 1, p] = -sin, -cos
    return out.reshape(2 * 128, NP * NZ)


@functools.cache
def y_table():
    ang = angles(kept(KY, NY), NY)
    return np.concatenate([np.cos(ang), np.sin(ang)], 0).astype(np.float32)


@functools.cache
def x_table():
    nx = NS * NP
    ang = angles(kept(KX, nx), nx)
    cos, sin = np.cos(ang).T / math.sqrt(nx), np.sin(ang).T / math.sqrt(nx)
    out = np.zeros((nx, 2, 2, KX), np.float32)
    out[:, 0, 0], out[:, 0, 1], out[:, 1, 0], out[:, 1, 1] = cos, -sin, sin, cos
    return out


@functools.cache
def x_forward():
    out = np.zeros((QL, NS * NP, 2, 2, QL, KX), np.float32)
    for ql in range(QL):
        out[ql, :, :, :, ql] = x_table()
    return out.reshape(QL, 256, 256)


@functools.cache
def x_inverse():
    out = np.zeros((QL, 2, QL, KX, NS * NP, 2), np.float32)
    for ql in range(QL):
        out[ql, :, ql] = x_table().transpose(2, 3, 0, 1)
    return out.reshape(QL, 256, 256)


def dot(left, right):
    return jnp.dot(left, right, preferred_element_type=F32)


def twice_gelu_slope(x):
    bell = jnp.exp2(x * x * (-0.5 * math.log2(math.e)) + math.log2(2.0 * 0.3989422804014327))
    return 1.0 + (lax.erf(x * 0.7071067811865476) + x * bell)


def analysis_kernel(go_hbm, pa_hbm, sw_hbm, za_hbm, cs_ref, send_ref, za_ref, go_ref, pa_ref, sw_ref, even_ref, odd_ref, proj_ref, rows_ref, go_sem, pa_sem, sw_sem, za_sem):
    def fetch(n):
        part = pl.ds(n * CB, CB)
        return (
            pltpu.make_async_copy(go_hbm.at[0, part], go_ref.at[part], go_sem.at[n]),
            pltpu.make_async_copy(pa_hbm.at[0, part], pa_ref.at[part], pa_sem.at[n]),
        )

    def slope(step, left_ref):
        for c in range(CB):
            for p in range(NP):
                at = step * CB + c
                value = go_ref[at, p].astype(F32) * twice_gelu_slope(pa_ref[at, p].astype(F32))
                left_ref[p // 2, c * NY : (c + 1) * NY, (p % 2) * NZ : (p % 2 + 1) * NZ] = value.astype(BF)

    def transform(step, left_ref):
        tz = (dot(left_ref[0], za_ref[:256]) + dot(left_ref[1], za_ref[256:])).astype(BF)
        for c in range(CB):
            both = dot(cs_ref[...], tz[c * NY : (c + 1) * NY])
            proj_ref[pl.ds(((step + 1) * CB + c) * KY, KY), :] = both[:KY, :128] + both[KY:, 128:]

    def weights(step):
        j = step // 2
        lanes = pl.ds(pl.multiple_of((step % 2) * 256, 256), 256)
        block = sw_ref[step // 4, pl.ds((j % 2) * 16, 16), :, lanes].astype(F32).reshape(128, 256)
        for h in range(2):
            turned = block[:, h * 128 : (h + 1) * 128].T
            for qh in range(2):
                first = ((step % 2) * 4 + h * 2 + qh) * KZ
                for ql in range(QL):
                    at = (qh * QL + ql) * KZ
                    rows_ref[pl.ds(first * 24 + 8 + j * 4 + ql, KZ, stride=24), :] = turned[at : at + KZ]

    za_copy = pltpu.make_async_copy(za_hbm, za_ref, za_sem)
    sw_copy = pltpu.make_async_copy(sw_hbm.at[0], sw_ref, sw_sem)
    for n in range(AHEAD):
        for copy in fetch(n):
            copy.start()
        if n == 0:
            za_copy.start()
            sw_copy.start()
    odd_ref[...] = jnp.zeros_like(odd_ref)

    @pl.loop(0, STEPS // 2)
    def _(pair):
        for half, (now, before) in enumerate(((even_ref, odd_ref), (odd_ref, even_ref))):
            step = pair * 2 + half

            @pl.when(step + AHEAD < STEPS)
            def _():
                for copy in fetch(step + AHEAD):
                    copy.start()

            for copy in fetch(step):
                copy.wait()
            if half == 0:

                @pl.when(pair == 0)
                def _():
                    za_copy.wait()
                    sw_copy.wait()

            slope(step, now)
            transform(step - 1, before)
            weights(step)

    transform(STEPS - 1, odd_ref)
    for qh in range(KY // QL):
        group = [proj_ref[pl.ds(CB * KY + qh * QL + ql, C, stride=KY), :] for ql in range(QL)]
        turned = jnp.concatenate(group, 0).T
        for kz in range(KZ):
            rows_ref[pl.ds((qh * KZ + kz) * 24, 8), :] = turned[kz * 8 : kz * 8 + 8]
    send_ref[...] = rows_ref[...].reshape(DEVS, 24, 128).astype(BF)


def analysis(grad_out, pre_act, spec_weight):
    hbm = pl.BlockSpec(memory_space=pl.ANY)
    vmem = pl.BlockSpec(memory_space=pltpu.VMEM)
    return pl.pallas_call(
        analysis_kernel,
        in_specs=[hbm, hbm, hbm, hbm, vmem],
        out_specs=vmem,
        out_shape=jax.ShapeDtypeStruct((DEVS, 24, 128), BF),
        scratch_shapes=[
            pltpu.VMEM((NP * NZ, 256), BF),
            pltpu.VMEM((C, NP, NY, NZ), BF),
            pltpu.VMEM((C, NP, NY, NZ), BF),
            pltpu.VMEM((2, C, SHARE, KY * KZ), BF),
            pltpu.VMEM((2, CB * NY, 2 * NZ), BF),
            pltpu.VMEM((2, CB * NY, 2 * NZ), BF),
            pltpu.VMEM(((C + CB) * KY, 128), F32),
            pltpu.VMEM((DEVS * 24, 128), F32),
            pltpu.SemaphoreType.DMA((STEPS,)),
            pltpu.SemaphoreType.DMA((STEPS,)),
            pltpu.SemaphoreType.DMA,
            pltpu.SemaphoreType.DMA,
        ],
        compiler_params=pltpu.CompilerParams(vmem_limit_bytes=VMEM_LIMIT),
        name="analysis",
    )(grad_out, pre_act, spec_weight, bf(z_analysis()), bf(y_table()))


YB = 16


def local_kernel(w_ref, go_ref, pa_ref, out_ref, wide_ref):
    @pl.when(pl.program_id(0) == 0)
    def _():
        row = lax.broadcasted_iota(jnp.int32, (C * 8, C), 0)
        pick = jnp.where(row // 8 == lax.broadcasted_iota(jnp.int32, (C * 8, C), 1), 1.0, 0.0).astype(BF)
        spread = dot(dot(pick, w_ref[...]).astype(BF), pick.T)
        row = lax.broadcasted_iota(jnp.int32, (C * 8, C * 8), 0)
        column = lax.broadcasted_iota(jnp.int32, (C * 8, C * 8), 1)
        wide_ref[...] = jnp.where(row % 8 == column % 8, 0.5 * spread, 0.0).astype(BF)

    for p in range(NP):
        block = go_ref[0, :, p].astype(F32) * twice_gelu_slope(pa_ref[0, :, p].astype(F32))
        right = jnp.concatenate([block[:, h * 8 : h * 8 + 8].reshape(C * 8, NZ) for h in range(2)], 1).astype(BF)
        full = dot(wide_ref[...], right)
        halves = [full[:, h * NZ : (h + 1) * NZ].reshape(C, 8, NZ) for h in range(2)]
        out_ref[:, p] = jnp.concatenate(halves, 1).astype(BF)


def local_map(w_local, grad_out, pre_act):
    spec = pl.BlockSpec((1, C, NP, YB, NZ), lambda n: (0, 0, 0, n, 0))
    return pl.pallas_call(
        local_kernel,
        grid=(NY // YB,),
        in_specs=[pl.BlockSpec((C, C), lambda n: (0, 0)), spec, spec],
        out_specs=pl.BlockSpec((C, NP, YB, NZ), lambda n: (0, 0, n, 0)),
        out_shape=jax.ShapeDtypeStruct((C, NP, NY, NZ), BF),
        scratch_shapes=[pltpu.VMEM((C * 8, C * 8), BF)],
        compiler_params=pltpu.CompilerParams(vmem_limit_bytes=VMEM_LIMIT),
        cost_estimate=pl.CostEstimate(flops=2 * C * C * 8 * NP * NY * NZ, bytes_accessed=12 << 20, transcendentals=0),
        name="local_map",
    )(w_local, grad_out, pre_act)


def mix_kernel(got_ref, wf_ref, wi_ref, send_ref, rows_ref, v_ref, out_ref, g_ref, back_ref):
    rows_ref[...] = got_ref[...].astype(F32).reshape(DEVS * 24, 128)
    for j in range(4):
        for og in range(NB):
            first = og * NS * 24 + 8 + j * 4
            group = [rows_ref[pl.ds(first + ql, KX, stride=24), :] for ql in range(QL)]
            at = (j * NB + og) * 128
            v_ref[at : at + 128, :] = jnp.concatenate(group, 0).T

    planes = []
    for b in range(NB):
        part = [rows_ref[pl.ds((b * NS + s) * 24, 8), :] for s in range(NS)]
        planes.append(jnp.concatenate(part, 0).T.astype(BF))
    grad = jnp.zeros((NB * C, 256), F32)
    for ql in range(QL):
        left = jnp.concatenate([planes[b][ql * C : (ql + 1) * C] for b in range(NB)], 0)
        grad = grad + dot(left, wf_ref[ql])
    g_ref[...] = grad

    turned = grad.T
    for r in range(2):
        for ql in range(QL):
            at = (r * QL + ql) * KX
            for og in range(NB):
                first = og * NS * 16 + 8 + r * QL + ql
                out_ref[pl.ds(first, KX, stride=16), :] = turned[at : at + KX]

    for ig in range(4):
        acc = [[jnp.zeros((8, 128), F32) for _ in range(2)] for _ in range(NB)]
        for o in range(C):
            at = (o // SHARE) * 128 + (ig % 2) * 64 + o % SHARE
            vr = v_ref[pl.ds((ig // 2) * 512 + at, 8, stride=SHARE), :]
            vi = v_ref[pl.ds((2 + ig // 2) * 512 + at, 8, stride=SHARE), :]
            for b in range(NB):
                gr = g_ref[pl.ds(b * C + o, 1), :128]
                gi = g_ref[pl.ds(b * C + o, 1), 128:]
                acc[b][0] = acc[b][0] + gr * vr + gi * vi
                acc[b][1] = acc[b][1] + gi * vr - gr * vi
        for b in range(NB):
            back_ref[b * C + ig * 8 : b * C + ig * 8 + 8, :] = jnp.concatenate(acc[b], 1)

    back = back_ref[...].astype(BF)
    outs = [dot(back, wi_ref[ql]) for ql in range(QL)]
    for b in range(NB):
        turned = jnp.concatenate([outs[ql][b * C : (b + 1) * C] for ql in range(QL)], 0).T
        for s in range(NS):
            out_ref[pl.ds((b * NS + s) * 16, 8), :] = turned[s * 8 : s * 8 + 8]
    send_ref[...] = out_ref[...].reshape(DEVS, 16, 128).astype(BF)


def mix(got):
    return pl.pallas_call(
        mix_kernel,
        out_shape=jax.ShapeDtypeStruct((DEVS, 16, 128), BF),
        scratch_shapes=[
            pltpu.VMEM((DEVS * 24, 128), F32),
            pltpu.VMEM((16 * 128, 128), F32),
            pltpu.VMEM((DEVS * 16, 128), F32),
            pltpu.VMEM((128, 256), F32),
            pltpu.VMEM((128, 256), F32),
        ],
        compiler_params=pltpu.CompilerParams(vmem_limit_bytes=16 << 20),
        name="mix",
    )(got, bf(x_forward()), bf(x_inverse()))


def synthesis_kernel(me_ref, got_ref, local_hbm, fm0, fm1, fm2, fm3, cs_ref, zs_ref, out_hbm, spec_hbm, rows_ref, x_ref, g_ref, u_ref, local_ref, out_ref, spec_ref, in_sem, out_sem, spec_sem):
    me = me_ref[0]

    def fetch(n):
        part = pl.ds(n * CB, CB)
        return pltpu.make_async_copy(local_hbm.at[part], local_ref.at[part], in_sem.at[n])

    def store(n):
        part = pl.ds(n * CB, CB)
        return pltpu.make_async_copy(out_ref.at[part], out_hbm.at[0, part], out_sem.at[n])

    def spec_store(n):
        part = pl.ds(n * CB, CB)
        return pltpu.make_async_copy(spec_ref.at[:, part], spec_hbm.at[0, :, part], spec_sem.at[n])

    for n in range(STEPS):
        fetch(n).start()
    rows_ref[...] = got_ref[...].astype(F32).reshape(DEVS * 16, 128)
    for qh in range(KY // QL):
        group = [rows_ref[pl.ds((qh * KZ + kz) * 16, 8), :] for kz in range(KZ)]
        turned = jnp.concatenate(group, 0).T
        for ql in range(QL):
            x_ref[pl.ds(qh * QL + ql, C, stride=KY), :] = turned[ql * C : (ql + 1) * C]
    for r in range(2):
        for tile in range(4):
            group = []
            for q in range(2 * QL):
                first = (tile * 2 + q // QL) * KZ * 16 + 8 + r * QL + q % QL
                group.append(rows_ref[pl.ds(first, KZ, stride=16), :])
            g_ref[r, :, tile * 128 : (tile + 1) * 128] = jnp.concatenate(group, 0).T
    for hop, fm in enumerate((fm0, fm1, fm2, fm3)):
        u_ref[hop] = fm[...].astype(F32)

    @pl.loop(0, STEPS)
    def _(step):
        fetch(step).wait()
        for pair in range(CB // 2):
            first = (step * CB + pair * 2) * KY
            xs = jnp.concatenate([x_ref[pl.ds(first, KY), :], x_ref[pl.ds(first + KY, KY), :]], 1)
            uv = dot(cs_ref[...], xs.astype(BF)).astype(BF)
            left = [
                jnp.concatenate([uv[:NY, k * 128 : k * 128 + 128], uv[NY:, k * 128 : k * 128 + 128]], 1)
                for k in range(2)
            ]
            full = dot(jnp.concatenate(left, 0), zs_ref[...])
            for k in range(2):
                c = step * CB + pair * 2 + k
                for p in range(NP):
                    total = full[k * NY : (k + 1) * NY, p * NZ : (p + 1) * NZ] + local_ref[c, p].astype(F32)
                    out_ref[c, p] = total.astype(BF)
        store(step).start()

        for k in range(CB):
            i = step * CB + k
            wr, wi = jnp.zeros((SHARE, KY * KZ), F32), jnp.zeros((SHARE, KY * KZ), F32)
            for hop in range(NB):
                at = pl.multiple_of((me ^ hop) * C + me * SHARE, SHARE)
                gr, gi = g_ref[0, pl.ds(at, SHARE), :], g_ref[1, pl.ds(at, SHARE), :]
                ur, ui = u_ref[hop, 0, pl.ds(i, 1), :], u_ref[hop, 1, pl.ds(i, 1), :]
                wr = wr + gr * ur + gi * ui
                wi = wi + gi * ur - gr * ui
            spec_ref[0, i] = wr
            spec_ref[1, i] = wi
        spec_store(step).start()

    for n in range(STEPS):
        store(n).wait()
        spec_store(n).wait()


def synthesis(me, got, local, fms):
    hbm = pl.BlockSpec(memory_space=pl.ANY)
    vmem = pl.BlockSpec(memory_space=pltpu.VMEM)
    table = y_table().reshape(2, KY, NY).transpose(0, 2, 1).reshape(2 * NY, KY)
    return pl.pallas_call(
        synthesis_kernel,
        in_specs=[pl.BlockSpec(memory_space=pltpu.SMEM), vmem, hbm, *[vmem] * NB, vmem, vmem],
        out_specs=[hbm, hbm],
        out_shape=[
            jax.ShapeDtypeStruct((1, C, NP, NY, NZ), BF),
            jax.ShapeDtypeStruct((1, 2, C, SHARE, KY * KZ), F32),
        ],
        scratch_shapes=[
            pltpu.VMEM((DEVS * 16, 128), F32),
            pltpu.VMEM((C * KY, 128), F32),
            pltpu.VMEM((2, 128, KY * KZ), F32),
            pltpu.VMEM((NB, 2, C, KY * KZ), F32),
            pltpu.VMEM((C, NP, NY, NZ), BF),
            pltpu.VMEM((C, NP, NY, NZ), BF),
            pltpu.VMEM((2, C, SHARE, KY * KZ), F32),
            pltpu.SemaphoreType.DMA((STEPS,)),
            pltpu.SemaphoreType.DMA((STEPS,)),
            pltpu.SemaphoreType.DMA((STEPS,)),
        ],
        compiler_params=pltpu.CompilerParams(vmem_limit_bytes=51 << 20),
        name="synthesis",
    )(me, got, local, *fms, bf(table), bf(z_synthesis()))


def shards(grad_out, pre_act, forward_modes, spec_weight, w_local):
    me = lax.axis_index("dp")
    send = analysis(grad_out, pre_act, spec_weight)
    send, grad_out, pre_act = lax.optimization_barrier((send, grad_out, pre_act))
    got = lax.all_to_all(send, ALL, 0, 0, tiled=True)
    local = local_map(w_local, grad_out, pre_act)
    got, local = lax.optimization_barrier((got, local))
    fm = forward_modes.reshape(2, C, KY * KZ)
    fms = [fm] + [lax.ppermute(fm, "dp", [(b, b ^ hop) for b in range(NB)]) for hop in range(1, NB)]
    got = lax.all_to_all(mix(got), ALL, 0, 0, tiled=True)
    return synthesis(me.reshape(1), got, local, fms)


def solution(mesh):
    return jax.shard_map(
        shards,
        mesh=mesh,
        in_specs=(
            P("dp", None, "slab", None, None),
            P("dp", None, "slab", None, None),
            P("dp", "slab", None, None, None),
            P("slab", None, None, "dp", None),
            P(),
        ),
        out_specs=(P("dp", None, "slab", None, None), P("slab", None, None, "dp", None)),
        check_vma=False,
    )
```

```python
import functools
import math

import jax
import jax.numpy as jnp
import numpy as np
from jax import lax
from jax.experimental import pallas as pl
from jax.experimental.pallas import tpu as pltpu
from jax.sharding import PartitionSpec as P

C = 32
NP = 4
NY = 128
NZ = 128
KX = 32
KY = 32
KZ = 16
NB = 4
NS = 32
QL = 4
SHARE = C // NB
DEVS = NB * NS
STEPS = 8
CB = C // STEPS
AHEAD = 2
SIZES = (8, 8, 8, 8)
STARTS = tuple(sum(SIZES[:n]) for n in range(len(SIZES)))
ALL = ("dp", "slab")
BF = jnp.bfloat16
F32 = jnp.float32
VMEM_LIMIT = 56 << 20


def kept(count, length):
    index = np.arange(count)
    return np.where(index < count // 2, index, length - count + index)


def angles(modes, length):
    return (modes[:, None] * np.arange(length)[None, :] % length) * (2.0 * math.pi / length)


def bf(table):
    return jnp.asarray(table, F32).astype(BF)


@functools.cache
def z_analysis():
    ang = angles(np.arange(KZ), NZ)
    weight = np.where(np.arange(KZ) == 0, 0.5, 1.0)[:, None] / math.sqrt(NY * NZ)
    real, imag = (np.cos(ang) * weight).T, (-np.sin(ang) * weight).T
    out = np.zeros((NP, NZ, 2, KZ, NP, 2), np.float32)
    for p in range(NP):
        out[p, :, 0, :, p, 0], out[p, :, 0, :, p, 1] = real, imag
        out[p, :, 1, :, p, 0], out[p, :, 1, :, p, 1] = imag, -real
    return out.reshape(NP * NZ, 2 * 128)


@functools.cache
def z_synthesis():
    ang = angles(np.arange(KZ), NZ)
    scale = 1.0 / math.sqrt(NY * NZ)
    cos, sin = np.cos(ang) * scale, np.sin(ang) * scale
    out = np.zeros((2, KZ, NP, 2, NP, NZ), np.float32)
    for p in range(NP):
        out[0, :, p, 0, p], out[0, :, p, 1, p] = cos, -sin
        out[1, :, p, 0, p], out[1, :, p, 1, p] = -sin, -cos
    return out.reshape(2 * 128, NP * NZ)


@functools.cache
def y_table():
    ang = angles(kept(KY, NY), NY)
    return np.concatenate([np.cos(ang), np.sin(ang)], 0).astype(np.float32)


@functools.cache
def x_table():
    nx = NS * NP
    ang = angles(kept(KX, nx), nx)
    cos, sin = np.cos(ang).T / math.sqrt(nx), np.sin(ang).T / math.sqrt(nx)
    out = np.zeros((nx, 2, 2, KX), np.float32)
    out[:, 0, 0], out[:, 0, 1], out[:, 1, 0], out[:, 1, 1] = cos, -sin, sin, cos
    return out


@functools.cache
def x_forward():
    out = np.zeros((QL, NS * NP, 2, 2, QL, KX), np.float32)
    for ql in range(QL):
        out[ql, :, :, :, ql] = x_table()
    return out.reshape(QL, 256, 256)


@functools.cache
def x_inverse():
    out = np.zeros((QL, 2, QL, KX, NS * NP, 2), np.float32)
    for ql in range(QL):
        out[ql, :, ql] = x_table().transpose(2, 3, 0, 1)
    return out.reshape(QL, 256, 256)


def dot(left, right):
    return jnp.dot(left, right, preferred_element_type=F32)


def twice_gelu_slope(x):
    bell = jnp.exp2(x * x * (-0.5 * math.log2(math.e)) + math.log2(2.0 * 0.3989422804014327))
    return 1.0 + (lax.erf(x * 0.7071067811865476) + x * bell)


def analysis_kernel(go_hbm, pa_hbm, sw_hbm, za_hbm, cs_ref, send_hbm, za_ref, go_ref, pa_ref, sw_ref, even_ref, odd_ref, proj_ref, rows_ref, send_ref, go_sem, pa_sem, sw_sem, za_sem, out_sem):
    def fetch(n):
        part = pl.ds(STARTS[n], SIZES[n])
        return (
            pltpu.make_async_copy(go_hbm.at[0, part], go_ref.at[part], go_sem.at[n]),
            pltpu.make_async_copy(pa_hbm.at[0, part], pa_ref.at[part], pa_sem.at[n]),
        )

    def slope(n, left_ref):
        for copy in fetch(n):
            copy.wait()
        for c in range(SIZES[n]):
            for p in range(NP):
                at = STARTS[n] + c
                value = go_ref[at, p].astype(F32) * twice_gelu_slope(pa_ref[at, p].astype(F32))
                left_ref[p // 2, c * NY : (c + 1) * NY, (p % 2) * NZ : (p % 2 + 1) * NZ] = value.astype(BF)

    def transform(n, left_ref):
        rows = SIZES[n] * NY
        tz = (dot(left_ref[0, :rows], za_ref[:256]) + dot(left_ref[1, :rows], za_ref[256:])).astype(BF)
        for c in range(SIZES[n]):
            both = dot(cs_ref[...], tz[c * NY : (c + 1) * NY])
            at = (STARTS[n] + c) * KY
            proj_ref[at : at + KY, :] = both[:KY, :128] + both[KY:, 128:]

    def weights(n):
        j, tile = n // 4, n % 4
        block = sw_ref[j // 2, (j % 2) * 16 : (j % 2) * 16 + 16, :, tile * 128 : tile * 128 + 128]
        turned = block.astype(F32).reshape(128, 128).T
        for qh in range(2):
            first = (tile * 2 + qh) * KZ
            for ql in range(QL):
                at = (qh * QL + ql) * KZ
                rows_ref[pl.ds(first * 24 + 8 + j * 4 + ql, KZ, stride=24), :] = turned[at : at + KZ]

    za_copy = pltpu.make_async_copy(za_hbm, za_ref, za_sem)
    sw_copy = pltpu.make_async_copy(sw_hbm.at[0], sw_ref, sw_sem)
    for n in range(AHEAD):
        for copy in fetch(n):
            copy.start()
        if n == 0:
            za_copy.start()
            sw_copy.start()
    buffers = (even_ref, odd_ref)
    for n in range(len(SIZES)):
        if n + AHEAD < len(SIZES):
            for copy in fetch(n + AHEAD):
                copy.start()
        if n == 1:
            za_copy.wait()
            sw_copy.wait()
        slope(n, buffers[n % 2])
        if n > 0:
            transform(n - 1, buffers[(n - 1) % 2])
            for tile in range(16):
                if tile * (len(SIZES) - 1) // 16 == n - 1:
                    weights(tile)
    transform(len(SIZES) - 1, buffers[(len(SIZES) - 1) % 2])

    outs = []
    for qh in range(KY // QL):
        group = [proj_ref[pl.ds(qh * QL + ql, C, stride=KY), :] for ql in range(QL)]
        turned = jnp.concatenate(group, 0).T
        for kz in range(KZ):
            rows_ref[pl.ds((qh * KZ + kz) * 24, 8), :] = turned[kz * 8 : kz * 8 + 8]
        part = pl.ds(qh * KZ, KZ)
        send_ref[part] = rows_ref[pl.ds(qh * KZ * 24, KZ * 24), :].reshape(KZ, 24, 128).astype(BF)
        outs.append(pltpu.make_async_copy(send_ref.at[part], send_hbm.at[part], out_sem.at[qh]))
        outs[-1].start()
    for copy in outs:
        copy.wait()


def analysis(grad_out, pre_act, spec_weight):
    hbm = pl.BlockSpec(memory_space=pl.ANY)
    vmem = pl.BlockSpec(memory_space=pltpu.VMEM)
    return pl.pallas_call(
        analysis_kernel,
        in_specs=[hbm, hbm, hbm, hbm, vmem],
        out_specs=hbm,
        out_shape=jax.ShapeDtypeStruct((DEVS, 24, 128), BF),
        scratch_shapes=[
            pltpu.VMEM((NP * NZ, 256), BF),
            pltpu.VMEM((C, NP, NY, NZ), BF),
            pltpu.VMEM((C, NP, NY, NZ), BF),
            pltpu.VMEM((2, C, SHARE, KY * KZ), BF),
            pltpu.VMEM((2, max(SIZES) * NY, 2 * NZ), BF),
            pltpu.VMEM((2, max(SIZES) * NY, 2 * NZ), BF),
            pltpu.VMEM((C * KY, 128), F32),
            pltpu.VMEM((DEVS * 24, 128), F32),
            pltpu.VMEM((DEVS, 24, 128), BF),
            pltpu.SemaphoreType.DMA((len(SIZES),)),
            pltpu.SemaphoreType.DMA((len(SIZES),)),
            pltpu.SemaphoreType.DMA,
            pltpu.SemaphoreType.DMA,
            pltpu.SemaphoreType.DMA((KY // QL,)),
        ],
        compiler_params=pltpu.CompilerParams(vmem_limit_bytes=VMEM_LIMIT),
        name="analysis",
    )(grad_out, pre_act, spec_weight, bf(z_analysis()), bf(y_table()))


YB = 32


def local_kernel(w_ref, go_ref, pa_ref, out_ref, wide_ref):
    @pl.when(pl.program_id(0) == 0)
    def _():
        row = lax.broadcasted_iota(jnp.int32, (C * 8, C), 0)
        pick = jnp.where(row // 8 == lax.broadcasted_iota(jnp.int32, (C * 8, C), 1), 1.0, 0.0).astype(BF)
        spread = dot(dot(pick, w_ref[...]).astype(BF), pick.T)
        row = lax.broadcasted_iota(jnp.int32, (C * 8, C * 8), 0)
        column = lax.broadcasted_iota(jnp.int32, (C * 8, C * 8), 1)
        wide_ref[...] = jnp.where(row % 8 == column % 8, 0.5 * spread, 0.0).astype(BF)

    for p in range(NP):
        block = go_ref[0, :, p].astype(F32) * twice_gelu_slope(pa_ref[0, :, p].astype(F32))
        right = jnp.concatenate([block[:, h * 8 : h * 8 + 8].reshape(C * 8, NZ) for h in range(YB // 8)], 1).astype(BF)
        full = dot(wide_ref[...], right)
        halves = [full[:, h * NZ : (h + 1) * NZ].reshape(C, 8, NZ) for h in range(YB // 8)]
        out_ref[:, p] = jnp.concatenate(halves, 1).astype(BF)


def local_map(w_local, grad_out, pre_act):
    spec = pl.BlockSpec((1, C, NP, YB, NZ), lambda n: (0, 0, 0, n, 0))
    return pl.pallas_call(
        local_kernel,
        grid=(NY // YB,),
        in_specs=[pl.BlockSpec((C, C), lambda n: (0, 0)), spec, spec],
        out_specs=pl.BlockSpec((C, NP, YB, NZ), lambda n: (0, 0, n, 0)),
        out_shape=jax.ShapeDtypeStruct((C, NP, NY, NZ), BF),
        scratch_shapes=[pltpu.VMEM((C * 8, C * 8), BF)],
        compiler_params=pltpu.CompilerParams(vmem_limit_bytes=VMEM_LIMIT),
        cost_estimate=pl.CostEstimate(flops=2 * C * C * 8 * NP * NY * NZ, bytes_accessed=12 << 20, transcendentals=0),
        name="local_map",
    )(w_local, grad_out, pre_act)


def mix_kernel(got_ref, wf_ref, wi_ref, send_ref, rows_ref, v_ref, out_ref, g_ref, back_ref):
    rows_ref[...] = got_ref[...].astype(F32).reshape(DEVS * 24, 128)
    for j in range(4):
        for og in range(NB):
            first = og * NS * 24 + 8 + j * 4
            group = [rows_ref[pl.ds(first + ql, KX, stride=24), :] for ql in range(QL)]
            at = (j * NB + og) * 128
            v_ref[at : at + 128, :] = jnp.concatenate(group, 0).T

    planes = []
    for b in range(NB):
        part = [rows_ref[pl.ds((b * NS + s) * 24, 8), :] for s in range(NS)]
        planes.append(jnp.concatenate(part, 0).T.astype(BF))
    grad = jnp.zeros((NB * C, 256), F32)
    for ql in range(QL):
        left = jnp.concatenate([planes[b][ql * C : (ql + 1) * C] for b in range(NB)], 0)
        grad = grad + dot(left, wf_ref[ql])
    g_ref[...] = grad

    turned = grad.T
    for r in range(2):
        for ql in range(QL):
            at = (r * QL + ql) * KX
            for og in range(NB):
                first = og * NS * 16 + 8 + r * QL + ql
                out_ref[pl.ds(first, KX, stride=16), :] = turned[at : at + KX]

    for ig in range(4):
        acc = [[jnp.zeros((8, 128), F32) for _ in range(2)] for _ in range(NB)]
        for o in range(C):
            at = (o // SHARE) * 128 + (ig % 2) * 64 + o % SHARE
            vr = v_ref[pl.ds((ig // 2) * 512 + at, 8, stride=SHARE), :]
            vi = v_ref[pl.ds((2 + ig // 2) * 512 + at, 8, stride=SHARE), :]
            for b in range(NB):
                gr = g_ref[pl.ds(b * C + o, 1), :128]
                gi = g_ref[pl.ds(b * C + o, 1), 128:]
                acc[b][0] = acc[b][0] + gr * vr + gi * vi
                acc[b][1] = acc[b][1] + gi * vr - gr * vi
        for b in range(NB):
            back_ref[b * C + ig * 8 : b * C + ig * 8 + 8, :] = jnp.concatenate(acc[b], 1)

    back = back_ref[...].astype(BF)
    outs = [dot(back, wi_ref[ql]) for ql in range(QL)]
    for b in range(NB):
        turned = jnp.concatenate([outs[ql][b * C : (b + 1) * C] for ql in range(QL)], 0).T
        for s in range(NS):
            out_ref[pl.ds((b * NS + s) * 16, 8), :] = turned[s * 8 : s * 8 + 8]
    send_ref[...] = out_ref[...].reshape(DEVS, 16, 128).astype(BF)


def mix(got):
    return pl.pallas_call(
        mix_kernel,
        out_shape=jax.ShapeDtypeStruct((DEVS, 16, 128), BF),
        scratch_shapes=[
            pltpu.VMEM((DEVS * 24, 128), F32),
            pltpu.VMEM((16 * 128, 128), F32),
            pltpu.VMEM((DEVS * 16, 128), F32),
            pltpu.VMEM((128, 256), F32),
            pltpu.VMEM((128, 256), F32),
        ],
        compiler_params=pltpu.CompilerParams(vmem_limit_bytes=16 << 20),
        name="mix",
    )(got, bf(x_forward()), bf(x_inverse()))


def synthesis_kernel(me_ref, got_ref, local_hbm, fm0, fm1, fm2, fm3, cs_ref, zs_ref, out_hbm, spec_hbm, rows_ref, x_ref, g_ref, u_ref, uv_ref, local_ref, out_ref, spec_ref, in_sem, out_sem, spec_sem):
    me = me_ref[0]

    def fetch(n):
        part = pl.ds(n * CB, CB)
        return pltpu.make_async_copy(local_hbm.at[part], local_ref.at[part], in_sem.at[n])

    def store(n):
        part = pl.ds(n * CB, CB)
        return pltpu.make_async_copy(out_ref.at[part], out_hbm.at[0, part], out_sem.at[n])

    def spec_store(n):
        part = pl.ds(n * CB, CB)
        return pltpu.make_async_copy(spec_ref.at[:, part], spec_hbm.at[0, :, part], spec_sem.at[n])

    for n in range(STEPS):
        fetch(n).start()
    rows_ref[...] = got_ref[...].astype(F32).reshape(DEVS * 16, 128)
    for qh in range(KY // QL):
        group = [rows_ref[pl.ds((qh * KZ + kz) * 16, 8), :] for kz in range(KZ)]
        turned = jnp.concatenate(group, 0).T
        for ql in range(QL):
            x_ref[pl.ds(qh * QL + ql, C, stride=KY), :] = turned[ql * C : (ql + 1) * C]
    for r in range(2):
        for tile in range(4):
            group = []
            for q in range(2 * QL):
                first = (tile * 2 + q // QL) * KZ * 16 + 8 + r * QL + q % QL
                group.append(rows_ref[pl.ds(first, KZ, stride=16), :])
            g_ref[r, :, tile * 128 : (tile + 1) * 128] = jnp.concatenate(group, 0).T
    for hop, fm in enumerate((fm0, fm1, fm2, fm3)):
        u_ref[hop] = fm[...].astype(F32)

    for pair in range(C // 2):
        first = pair * 2 * KY
        xs = jnp.concatenate([x_ref[first : first + KY, :], x_ref[first + KY : first + 2 * KY, :]], 1)
        uv = dot(cs_ref[...], xs.astype(BF)).astype(BF)
        for k in range(2):
            uv_ref[pair * 2 + k, :, :128] = uv[:NY, k * 128 : k * 128 + 128]
            uv_ref[pair * 2 + k, :, 128:] = uv[NY:, k * 128 : k * 128 + 128]

    @pl.loop(0, STEPS)
    def _(step):
        fetch(step).wait()
        left = uv_ref[pl.ds(step * CB, CB)].reshape(CB * NY, 256)
        for p in range(NP):
            if p % 2 == 0:
                wide = dot(left, zs_ref[:, p * NZ : (p + 2) * NZ])
            full = wide[:, (p % 2) * NZ : (p % 2 + 1) * NZ]
            for k in range(CB):
                c = step * CB + k
                total = full[k * NY : (k + 1) * NY] + local_ref[c, p].astype(F32)
                out_ref[c, p] = total.astype(BF)
        store(step).start()

        for k in range(CB):
            i = step * CB + k
            wr, wi = jnp.zeros((SHARE, KY * KZ), F32), jnp.zeros((SHARE, KY * KZ), F32)
            for hop in range(NB):
                at = pl.multiple_of((me ^ hop) * C + me * SHARE, SHARE)
                gr, gi = g_ref[0, pl.ds(at, SHARE), :], g_ref[1, pl.ds(at, SHARE), :]
                ur, ui = u_ref[hop, 0, pl.ds(i, 1), :], u_ref[hop, 1, pl.ds(i, 1), :]
                wr = wr + gr * ur + gi * ui
                wi = wi + gi * ur - gr * ui
            spec_ref[0, i] = wr
            spec_ref[1, i] = wi
        spec_store(step).start()

    for n in range(STEPS):
        store(n).wait()
        spec_store(n).wait()


def synthesis(me, got, local, fms):
    hbm = pl.BlockSpec(memory_space=pl.ANY)
    vmem = pl.BlockSpec(memory_space=pltpu.VMEM)
    table = y_table().reshape(2, KY, NY).transpose(0, 2, 1).reshape(2 * NY, KY)
    return pl.pallas_call(
        synthesis_kernel,
        in_specs=[pl.BlockSpec(memory_space=pltpu.SMEM), vmem, hbm, *[vmem] * NB, vmem, vmem],
        out_specs=[hbm, hbm],
        out_shape=[
            jax.ShapeDtypeStruct((1, C, NP, NY, NZ), BF),
            jax.ShapeDtypeStruct((1, 2, C, SHARE, KY * KZ), F32),
        ],
        scratch_shapes=[
            pltpu.VMEM((DEVS * 16, 128), F32),
            pltpu.VMEM((C * KY, 128), F32),
            pltpu.VMEM((2, 128, KY * KZ), F32),
            pltpu.VMEM((NB, 2, C, KY * KZ), F32),
            pltpu.VMEM((C, NY, 256), BF),
            pltpu.VMEM((C, NP, NY, NZ), BF),
            pltpu.VMEM((C, NP, NY, NZ), BF),
            pltpu.VMEM((2, C, SHARE, KY * KZ), F32),
            pltpu.SemaphoreType.DMA((STEPS,)),
            pltpu.SemaphoreType.DMA((STEPS,)),
            pltpu.SemaphoreType.DMA((STEPS,)),
        ],
        compiler_params=pltpu.CompilerParams(vmem_limit_bytes=51 << 20),
        name="synthesis",
    )(me, got, local, *fms, bf(table), bf(z_synthesis()))


def shards(grad_out, pre_act, forward_modes, spec_weight, w_local):
    me = lax.axis_index("dp")
    send = analysis(grad_out, pre_act, spec_weight)
    send, grad_out, pre_act = lax.optimization_barrier((send, grad_out, pre_act))
    got = lax.all_to_all(send, ALL, 0, 0, tiled=True)
    local = local_map(w_local, grad_out, pre_act)
    got, local = lax.optimization_barrier((got, local))
    fm = forward_modes.reshape(2, C, KY * KZ)
    fms = [fm] + [lax.ppermute(fm, "dp", [(b, b ^ hop) for b in range(NB)]) for hop in range(1, NB)]
    got = lax.all_to_all(mix(got), ALL, 0, 0, tiled=True)
    return synthesis(me.reshape(1), got, local, fms)


def solution(mesh):
    return jax.shard_map(
        shards,
        mesh=mesh,
        in_specs=(
            P("dp", None, "slab", None, None),
            P("dp", None, "slab", None, None),
            P("dp", "slab", None, None, None),
            P("slab", None, None, "dp", None),
            P(),
        ),
        out_specs=(P("dp", None, "slab", None, None), P("slab", None, None, "dp", None)),
        check_vma=False,
    )
```

```python
import functools
import math

import jax
import jax.numpy as jnp
import numpy as np
from jax import lax
from jax.experimental import pallas as pl
from jax.experimental.pallas import tpu as pltpu
from jax.sharding import PartitionSpec as P

C = 32
NP = 4
NY = 128
NZ = 128
KX = 32
KY = 32
KZ = 16
NB = 4
NS = 32
QL = 4
SHARE = C // NB
DEVS = NB * NS
STEPS = 8
CB = C // STEPS
AHEAD = 2
SIZES = (8, 8, 8, 8)
STARTS = tuple(sum(SIZES[:n]) for n in range(len(SIZES)))
ALL = ("dp", "slab")
BACK = 10
BF = jnp.bfloat16
F32 = jnp.float32
VMEM_LIMIT = 56 << 20


def kept(count, length):
    index = np.arange(count)
    return np.where(index < count // 2, index, length - count + index)


def angles(modes, length):
    return (modes[:, None] * np.arange(length)[None, :] % length) * (2.0 * math.pi / length)


def bf(table):
    return jnp.asarray(table, F32).astype(BF)


@functools.cache
def z_analysis():
    ang = angles(np.arange(KZ), NZ)
    weight = np.where(np.arange(KZ) == 0, 0.5, 1.0)[:, None] / math.sqrt(NY * NZ)
    real, imag = (np.cos(ang) * weight).T, (-np.sin(ang) * weight).T
    out = np.zeros((NP, NZ, 2, KZ, NP, 2), np.float32)
    for p in range(NP):
        out[p, :, 0, :, p, 0], out[p, :, 0, :, p, 1] = real, imag
        out[p, :, 1, :, p, 0], out[p, :, 1, :, p, 1] = imag, -real
    return out.reshape(NP * NZ, 2 * 128)


@functools.cache
def z_synthesis():
    ang = angles(np.arange(KZ), NZ)
    scale = 1.0 / math.sqrt(NY * NZ)
    cos, sin = np.cos(ang) * scale, np.sin(ang) * scale
    out = np.zeros((2, KZ, NP, 2, NP, NZ), np.float32)
    for p in range(NP):
        out[0, :, p, 0, p], out[0, :, p, 1, p] = cos, -sin
        out[1, :, p, 0, p], out[1, :, p, 1, p] = -sin, -cos
    return out.reshape(2 * 128, NP * NZ)


@functools.cache
def y_table():
    ang = angles(kept(KY, NY), NY)
    return np.concatenate([np.cos(ang), np.sin(ang)], 0).astype(np.float32)


@functools.cache
def x_table():
    nx = NS * NP
    ang = angles(kept(KX, nx), nx)
    cos, sin = np.cos(ang).T / math.sqrt(nx), np.sin(ang).T / math.sqrt(nx)
    out = np.zeros((nx, 2, 2, KX), np.float32)
    out[:, 0, 0], out[:, 0, 1], out[:, 1, 0], out[:, 1, 1] = cos, -sin, sin, cos
    return out


@functools.cache
def x_forward():
    out = np.zeros((QL, NS * NP, 2, 2, QL, KX), np.float32)
    for ql in range(QL):
        out[ql, :, :, :, ql] = x_table()
    return out.reshape(QL, 256, 256)


@functools.cache
def x_inverse():
    out = np.zeros((QL, 2, QL, KX, NS * NP, 2), np.float32)
    for ql in range(QL):
        out[ql, :, ql] = x_table().transpose(2, 3, 0, 1)
    return out.reshape(QL, 256, 256)


def dot(left, right):
    return jnp.dot(left, right, preferred_element_type=F32)


def twice_gelu_slope(x):
    u = x * math.sqrt(0.5 * math.log2(math.e))
    bell = jnp.exp2(math.log2(2.0 * 0.3989422804014327) - u * u)
    return 1.0 + (lax.erf(x * 0.7071067811865476) + x * bell)


def analysis_kernel(go_hbm, pa_hbm, sw_hbm, za_hbm, cs_ref, send_hbm, za_ref, go_ref, pa_ref, sw_ref, even_ref, odd_ref, proj_ref, rows_ref, send_ref, go_sem, pa_sem, sw_sem, za_sem, out_sem):
    def fetch(n):
        part = pl.ds(STARTS[n], SIZES[n])
        return (
            pltpu.make_async_copy(go_hbm.at[0, part], go_ref.at[part], go_sem.at[n]),
            pltpu.make_async_copy(pa_hbm.at[0, part], pa_ref.at[part], pa_sem.at[n]),
        )

    def slope(n, left_ref):
        for copy in fetch(n):
            copy.wait()
        for c in range(SIZES[n]):
            for p in range(NP):
                at = STARTS[n] + c
                value = go_ref[at, p].astype(F32) * twice_gelu_slope(pa_ref[at, p].astype(F32))
                left_ref[p // 2, c * NY : (c + 1) * NY, (p % 2) * NZ : (p % 2 + 1) * NZ] = value.astype(BF)

    def transform(n, left_ref):
        rows = SIZES[n] * NY
        tz = (dot(left_ref[0, :rows], za_ref[:256]) + dot(left_ref[1, :rows], za_ref[256:])).astype(BF)
        for c in range(SIZES[n]):
            both = dot(cs_ref[...], tz[c * NY : (c + 1) * NY])
            at = (STARTS[n] + c) * KY
            proj_ref[at : at + KY, :] = both[:KY, :128] + both[KY:, 128:]

    def weights(n):
        j, tile = n // 4, n % 4
        block = sw_ref[j // 2, (j % 2) * 16 : (j % 2) * 16 + 16, :, tile * 128 : tile * 128 + 128]
        turned = block.astype(F32).reshape(128, 128).T
        for qh in range(2):
            first = (tile * 2 + qh) * KZ
            for ql in range(QL):
                at = (qh * QL + ql) * KZ
                rows_ref[pl.ds(first * 24 + 8 + j * 4 + ql, KZ, stride=24), :] = turned[at : at + KZ]

    za_copy = pltpu.make_async_copy(za_hbm, za_ref, za_sem)
    sw_copy = pltpu.make_async_copy(sw_hbm.at[0], sw_ref, sw_sem)
    for n in range(AHEAD):
        for copy in fetch(n):
            copy.start()
        if n == 0:
            za_copy.start()
            sw_copy.start()
    buffers = (even_ref, odd_ref)
    for n in range(len(SIZES)):
        if n + AHEAD < len(SIZES):
            for copy in fetch(n + AHEAD):
                copy.start()
        if n == 1:
            za_copy.wait()
            sw_copy.wait()
        slope(n, buffers[n % 2])
        if n > 0:
            transform(n - 1, buffers[(n - 1) % 2])
            for tile in range(16):
                if tile * (len(SIZES) - 1) // 16 == n - 1:
                    weights(tile)
    transform(len(SIZES) - 1, buffers[(len(SIZES) - 1) % 2])

    outs = []
    for qh in range(KY // QL):
        group = [proj_ref[pl.ds(qh * QL + ql, C, stride=KY), :] for ql in range(QL)]
        turned = jnp.concatenate(group, 0).T
        for kz in range(KZ):
            rows_ref[pl.ds((qh * KZ + kz) * 24, 8), :] = turned[kz * 8 : kz * 8 + 8]
        part = pl.ds(qh * KZ, KZ)
        send_ref[part] = rows_ref[pl.ds(qh * KZ * 24, KZ * 24), :].reshape(KZ, 24, 128).astype(BF)
        outs.append(pltpu.make_async_copy(send_ref.at[part], send_hbm.at[part], out_sem.at[qh]))
        outs[-1].start()
    for copy in outs:
        copy.wait()


def analysis(grad_out, pre_act, spec_weight):
    hbm = pl.BlockSpec(memory_space=pl.ANY)
    vmem = pl.BlockSpec(memory_space=pltpu.VMEM)
    return pl.pallas_call(
        analysis_kernel,
        in_specs=[hbm, hbm, hbm, hbm, vmem],
        out_specs=hbm,
        out_shape=jax.ShapeDtypeStruct((DEVS, 24, 128), BF),
        scratch_shapes=[
            pltpu.VMEM((NP * NZ, 256), BF),
            pltpu.VMEM((C, NP, NY, NZ), BF),
            pltpu.VMEM((C, NP, NY, NZ), BF),
            pltpu.VMEM((2, C, SHARE, KY * KZ), BF),
            pltpu.VMEM((2, max(SIZES) * NY, 2 * NZ), BF),
            pltpu.VMEM((2, max(SIZES) * NY, 2 * NZ), BF),
            pltpu.VMEM((C * KY, 128), F32),
            pltpu.VMEM((DEVS * 24, 128), F32),
            pltpu.VMEM((DEVS, 24, 128), BF),
            pltpu.SemaphoreType.DMA((len(SIZES),)),
            pltpu.SemaphoreType.DMA((len(SIZES),)),
            pltpu.SemaphoreType.DMA,
            pltpu.SemaphoreType.DMA,
            pltpu.SemaphoreType.DMA((KY // QL,)),
        ],
        compiler_params=pltpu.CompilerParams(vmem_limit_bytes=VMEM_LIMIT),
        name="analysis",
    )(grad_out, pre_act, spec_weight, bf(z_analysis()), bf(y_table()))


YB = 32


def local_kernel(w_ref, go_ref, pa_ref, out_ref, wide_ref):
    @pl.when(pl.program_id(0) == 0)
    def _():
        row = lax.broadcasted_iota(jnp.int32, (C * 8, C), 0)
        pick = jnp.where(row // 8 == lax.broadcasted_iota(jnp.int32, (C * 8, C), 1), 1.0, 0.0).astype(BF)
        spread = dot(dot(pick, w_ref[...]).astype(BF), pick.T)
        row = lax.broadcasted_iota(jnp.int32, (C * 8, C * 8), 0)
        column = lax.broadcasted_iota(jnp.int32, (C * 8, C * 8), 1)
        wide_ref[...] = jnp.where(row % 8 == column % 8, 0.5 * spread, 0.0).astype(BF)

    for p in range(NP):
        block = go_ref[0, :, p].astype(F32) * twice_gelu_slope(pa_ref[0, :, p].astype(F32))
        right = jnp.concatenate([block[:, h * 8 : h * 8 + 8].reshape(C * 8, NZ) for h in range(YB // 8)], 1).astype(BF)
        full = dot(wide_ref[...], right)
        halves = [full[:, h * NZ : (h + 1) * NZ].reshape(C, 8, NZ) for h in range(YB // 8)]
        out_ref[:, p] = jnp.concatenate(halves, 1).astype(BF)


def local_map(w_local, grad_out, pre_act):
    spec = pl.BlockSpec((1, C, NP, YB, NZ), lambda n: (0, 0, 0, n, 0))
    return pl.pallas_call(
        local_kernel,
        grid=(NY // YB,),
        in_specs=[pl.BlockSpec((C, C), lambda n: (0, 0)), spec, spec],
        out_specs=pl.BlockSpec((C, NP, YB, NZ), lambda n: (0, 0, n, 0)),
        out_shape=jax.ShapeDtypeStruct((C, NP, NY, NZ), BF),
        scratch_shapes=[pltpu.VMEM((C * 8, C * 8), BF)],
        compiler_params=pltpu.CompilerParams(vmem_limit_bytes=VMEM_LIMIT),
        cost_estimate=pl.CostEstimate(flops=2 * C * C * 8 * NP * NY * NZ, bytes_accessed=12 << 20, transcendentals=0),
        name="local_map",
    )(w_local, grad_out, pre_act)


def mix_kernel(got_ref, wf_ref, wi_ref, send_hbm, rows_ref, v_ref, out_ref, g_ref, back_ref, send_ref, out_sem):
    rows_ref[...] = got_ref[...].astype(F32).reshape(DEVS * 24, 128)
    for j in range(4):
        for og in range(NB):
            first = og * NS * 24 + 8 + j * 4
            group = [rows_ref[pl.ds(first + ql, KX, stride=24), :] for ql in range(QL)]
            at = (j * NB + og) * 128
            v_ref[at : at + 128, :] = jnp.concatenate(group, 0).T

    planes = []
    for b in range(NB):
        part = [rows_ref[pl.ds((b * NS + s) * 24, 8), :] for s in range(NS)]
        planes.append(jnp.concatenate(part, 0).T.astype(BF))
    grad = jnp.zeros((NB * C, 256), F32)
    for ql in range(QL):
        left = jnp.concatenate([planes[b][ql * C : (ql + 1) * C] for b in range(NB)], 0)
        grad = grad + dot(left, wf_ref[ql])
    g_ref[...] = grad

    for og in range(NB):
        own = [grad[b * C + og * SHARE : b * C + (og + 1) * SHARE] for b in range(NB)]
        own = jnp.concatenate(own, 0)
        for r in range(2):
            part = [own[:, (r * QL + ql) * KX : (r * QL + ql + 1) * KX] for ql in range(QL)]
            turned = jnp.concatenate(part, 0).T
            out_ref[pl.ds(og * NS * BACK + 8 + r, KX, stride=BACK), :] = turned

    for ig in range(4):
        acc = [[jnp.zeros((8, 128), F32) for _ in range(2)] for _ in range(NB)]
        for o in range(C):
            at = (o // SHARE) * 128 + (ig % 2) * 64 + o % SHARE
            vr = v_ref[pl.ds((ig // 2) * 512 + at, 8, stride=SHARE), :]
            vi = v_ref[pl.ds((2 + ig // 2) * 512 + at, 8, stride=SHARE), :]
            for b in range(NB):
                gr = g_ref[pl.ds(b * C + o, 1), :128]
                gi = g_ref[pl.ds(b * C + o, 1), 128:]
                acc[b][0] = acc[b][0] + gr * vr + gi * vi
                acc[b][1] = acc[b][1] + gi * vr - gr * vi
        for b in range(NB):
            back_ref[b * C + ig * 8 : b * C + ig * 8 + 8, :] = jnp.concatenate(acc[b], 1)

    back = back_ref[...].astype(BF)
    outs = [dot(back, wi_ref[ql]) for ql in range(QL)]
    copies = []
    for b in range(NB):
        turned = jnp.concatenate([outs[ql][b * C : (b + 1) * C] for ql in range(QL)], 0).T
        for s in range(NS):
            out_ref[pl.ds((b * NS + s) * BACK, 8), :] = turned[s * 8 : s * 8 + 8]
        part = pl.ds(b * NS * BACK, NS * BACK)
        send_ref[part] = out_ref[part, :].astype(BF)
        copies.append(pltpu.make_async_copy(send_ref.at[part], send_hbm.at[part], out_sem.at[b]))
        copies[-1].start()
    for copy in copies:
        copy.wait()


def mix(got):
    return pl.pallas_call(
        mix_kernel,
        in_specs=[pl.BlockSpec(memory_space=pltpu.VMEM)] * 3,
        out_specs=pl.BlockSpec(memory_space=pl.ANY),
        out_shape=jax.ShapeDtypeStruct((DEVS * BACK, 128), BF),
        scratch_shapes=[
            pltpu.VMEM((DEVS * 24, 128), F32),
            pltpu.VMEM((16 * 128, 128), F32),
            pltpu.VMEM((DEVS * BACK, 128), F32),
            pltpu.VMEM((128, 256), F32),
            pltpu.VMEM((128, 256), F32),
            pltpu.VMEM((DEVS * BACK, 128), BF),
            pltpu.SemaphoreType.DMA((NB,)),
        ],
        compiler_params=pltpu.CompilerParams(vmem_limit_bytes=16 << 20),
        name="mix",
    )(got, bf(x_forward()), bf(x_inverse()))


def synthesis_kernel(me_ref, got_ref, local_hbm, fm0, fm1, fm2, fm3, cs_ref, zs_ref, out_hbm, spec_hbm, rows_ref, x_ref, g_ref, u_ref, uv_ref, local_ref, out_ref, spec_ref, in_sem, out_sem, spec_sem):
    me = me_ref[0]

    def fetch(n):
        part = pl.ds(n * CB, CB)
        return pltpu.make_async_copy(local_hbm.at[part], local_ref.at[part], in_sem.at[n])

    def store(n):
        part = pl.ds(n * CB, CB)
        return pltpu.make_async_copy(out_ref.at[part], out_hbm.at[0, part], out_sem.at[n])

    def spec_store(n):
        part = pl.ds(n * CB, CB)
        return pltpu.make_async_copy(spec_ref.at[:, part], spec_hbm.at[0, :, part], spec_sem.at[n])

    for n in range(STEPS):
        fetch(n).start()
    rows_ref[...] = got_ref[...].astype(F32)
    for qh in range(KY // QL):
        group = [rows_ref[pl.ds((qh * KZ + kz) * BACK, 8), :] for kz in range(KZ)]
        turned = jnp.concatenate(group, 0).T
        for ql in range(QL):
            x_ref[pl.ds(qh * QL + ql, C, stride=KY), :] = turned[ql * C : (ql + 1) * C]
    for r in range(2):
        for tile in range(4):
            group = []
            for qh in range(tile * 2, tile * 2 + 2):
                row = rows_ref[pl.ds(qh * KZ * BACK + 8 + r, KZ, stride=BACK), :]
                group += [row[:, ql * 32 : (ql + 1) * 32] for ql in range(QL)]
            g_ref[r, :, tile * 128 : (tile + 1) * 128] = jnp.concatenate(group, 0).T
    for hop, fm in enumerate((fm0, fm1, fm2, fm3)):
        u_ref[hop] = fm[...].astype(F32)

    for pair in range(C // 2):
        first = pair * 2 * KY
        xs = jnp.concatenate([x_ref[first : first + KY, :], x_ref[first + KY : first + 2 * KY, :]], 1)
        uv = dot(cs_ref[...], xs.astype(BF)).astype(BF)
        for k in range(2):
            uv_ref[pair * 2 + k, :, :128] = uv[:NY, k * 128 : k * 128 + 128]
            uv_ref[pair * 2 + k, :, 128:] = uv[NY:, k * 128 : k * 128 + 128]

    @pl.loop(0, STEPS)
    def _(step):
        fetch(step).wait()
        left = uv_ref[pl.ds(step * CB, CB)].reshape(CB * NY, 256)
        for p in range(NP):
            if p % 2 == 0:
                wide = dot(left, zs_ref[:, p * NZ : (p + 2) * NZ])
            full = wide[:, (p % 2) * NZ : (p % 2 + 1) * NZ]
            for k in range(CB):
                c = step * CB + k
                total = full[k * NY : (k + 1) * NY] + local_ref[c, p].astype(F32)
                out_ref[c, p] = total.astype(BF)
        store(step).start()

        for k in range(CB):
            i = step * CB + k
            wr, wi = jnp.zeros((SHARE, KY * KZ), F32), jnp.zeros((SHARE, KY * KZ), F32)
            for hop in range(NB):
                at = pl.multiple_of((me ^ hop) * SHARE, SHARE)
                gr, gi = g_ref[0, pl.ds(at, SHARE), :], g_ref[1, pl.ds(at, SHARE), :]
                ur, ui = u_ref[hop, 0, pl.ds(i, 1), :], u_ref[hop, 1, pl.ds(i, 1), :]
                wr = wr + gr * ur + gi * ui
                wi = wi + gi * ur - gr * ui
            spec_ref[0, i] = wr
            spec_ref[1, i] = wi
        spec_store(step).start()

    for n in range(STEPS):
        store(n).wait()
        spec_store(n).wait()


def synthesis(me, got, local, fms):
    hbm = pl.BlockSpec(memory_space=pl.ANY)
    vmem = pl.BlockSpec(memory_space=pltpu.VMEM)
    table = y_table().reshape(2, KY, NY).transpose(0, 2, 1).reshape(2 * NY, KY)
    return pl.pallas_call(
        synthesis_kernel,
        in_specs=[pl.BlockSpec(memory_space=pltpu.SMEM), vmem, hbm, *[vmem] * NB, vmem, vmem],
        out_specs=[hbm, hbm],
        out_shape=[
            jax.ShapeDtypeStruct((1, C, NP, NY, NZ), BF),
            jax.ShapeDtypeStruct((1, 2, C, SHARE, KY * KZ), F32),
        ],
        scratch_shapes=[
            pltpu.VMEM((DEVS * BACK, 128), F32),
            pltpu.VMEM((C * KY, 128), F32),
            pltpu.VMEM((2, NB * SHARE, KY * KZ), F32),
            pltpu.VMEM((NB, 2, C, KY * KZ), F32),
            pltpu.VMEM((C, NY, 256), BF),
            pltpu.VMEM((C, NP, NY, NZ), BF),
            pltpu.VMEM((C, NP, NY, NZ), BF),
            pltpu.VMEM((2, C, SHARE, KY * KZ), F32),
            pltpu.SemaphoreType.DMA((STEPS,)),
            pltpu.SemaphoreType.DMA((STEPS,)),
            pltpu.SemaphoreType.DMA((STEPS,)),
        ],
        compiler_params=pltpu.CompilerParams(vmem_limit_bytes=51 << 20),
        name="synthesis",
    )(me, got, local, *fms, bf(table), bf(z_synthesis()))


def shards(grad_out, pre_act, forward_modes, spec_weight, w_local):
    me = lax.axis_index("dp")
    send = analysis(grad_out, pre_act, spec_weight)
    send, grad_out, pre_act = lax.optimization_barrier((send, grad_out, pre_act))
    got = lax.all_to_all(send, ALL, 0, 0, tiled=True)
    local = local_map(w_local, grad_out, pre_act)
    got, local = lax.optimization_barrier((got, local))
    fm = forward_modes.reshape(2, C, KY * KZ)
    fms = [fm] + [lax.ppermute(fm, "dp", [(b, b ^ hop) for b in range(NB)]) for hop in range(1, NB)]
    back = mix(got).reshape(DEVS, BACK // 2, 2, 128)
    back = lax.all_to_all(back, ALL, 0, 0, tiled=True).reshape(DEVS * BACK, 128)
    return synthesis(me.reshape(1), back, local, fms)


def solution(mesh):
    return jax.shard_map(
        shards,
        mesh=mesh,
        in_specs=(
            P("dp", None, "slab", None, None),
            P("dp", None, "slab", None, None),
            P("dp", "slab", None, None, None),
            P("slab", None, None, "dp", None),
            P(),
        ),
        out_specs=(P("dp", None, "slab", None, None), P("slab", None, None, "dp", None)),
        check_vma=False,
    )
```
